32 devices in a mesh: groups: 2 (over y), seq: 4 (over z), queue: 4 (over x, core).
Axes of the slice: x: 2, y: 2, z: 4, core: 2. Of those that a mesh axis runs over, the one named last changes fastest.
Arguments:
- query_rows: bfloat16 [8, 512, 4096], P(('groups', 'queue'), 'seq'), parts along dimension 0, may hold values from -8 to 8
- key_rows: bfloat16 [8, 512, 4096], P(('groups', 'queue'), 'seq'), parts along dimension 0, may hold values from -8 to 8
- value_rows: bfloat16 [8, 512, 4096], P(('groups', 'queue'), 'seq'), parts along dimension 0, may hold values from -6 to 6
- hidden_state: bfloat16 [8, 512, 5120], P(('groups', 'queue'), 'seq'), parts along dimension 0, may hold values from -6 to 6
- modulation: float32 [8, 2, 5120], P(('groups', 'queue')), parts along dimension 0, may hold values from -4 to 4
- head_weight: bfloat16 [5120, 64], replicated, may hold values from -0.078125 to 0.078125
- latents: float32 [8, 512, 64], P(('groups', 'queue'), 'seq'), parts along dimension 0, may hold values from -6 to 6
- time_index: int32 [8], P(('groups', 'queue')), parts along dimension 0, may hold values from 1 to 8, as said below
- live_counts: int32 [32, 4], replicated, may hold values from 1 to 4, as said below
- block_lists: int32 [32, 4, 4], replicated, may hold values from 0 to 3, as said below
Outputs:
- attention_out: bfloat16 [8, 512, 4096], P(('groups', 'queue'), 'seq'), parts along dimension 0
- queue_next: float32 [8, 512, 64], P(('groups', 'queue'), 'seq'), parts along dimension 0
The draws below stay inside these ranges and needn't reach their ends.
There are 2 independent parts, one for each index of `groups`. The reference program is written for one: setup_inputs(seed, part) draws one part's arguments, and reference() takes and returns one part's arrays. A program takes and returns all parts, laid end to end along the dimension named above; an argument that names none is the same for every part. Nothing has to cross between parts.
Inputs may be any that keep to these rules, and one draw needn't show every extreme that they name: live_counts[h, b] leading entries of block_lists[h, b] are attended; 4 is reached in every draw. `block_lists`: for each head and query block the 4 entries are distinct block numbers, the first being the query block itself. `time_index`: strictly rising along the queue; the first position is at 1 and the last at 8.
All inputs are finite; a program needn't handle non-finite values.
Results may differ from the reference program's by a relative error of at most 0.0055.
Values may be sent and summed in bfloat16 or wider, within the bound.
A program may use at most 64 MiB of HBM per device.

```python
import jax
import jax.numpy as jnp
from jax import lax

D = 5120
HEADS = 32
HDIM = 128
LATENT = 64
BLK = 128
STEPS = 8
TOKENS = 512
QBLOCKS = 4
KMAX = 4
QUEUE = 4


def paired_fields(key):
    shape = (QUEUE, TOKENS, HEADS * HDIM)
    query_field = jnp.clip(jax.random.normal(jax.random.fold_in(key, 11), shape, jnp.float32), -6.0, 6.0)
    key_field = jnp.clip(jax.random.normal(jax.random.fold_in(key, 12), shape, jnp.float32), -6.0, 6.0)
    return (query_field, key_field)


def draw_query_rows(key, part):
    return paired_fields(key)[0].astype(jnp.bfloat16)


def draw_key_rows(key, part):
    return paired_fields(key)[1].astype(jnp.bfloat16)


def draw_time_index(key, part):
    middle = jnp.sort(jax.random.permutation(key, STEPS - 2)[:QUEUE - 2]) + 2
    values = jnp.concatenate([jnp.array([1], jnp.int32), middle.astype(jnp.int32), jnp.array([STEPS], jnp.int32)])
    return values.astype(jnp.int32)


def draw_live_counts(key, part):
    lowest = max(KMAX // 4, 1)
    upper = max(KMAX // 2, lowest)
    heavy = jax.random.randint(jax.random.fold_in(key, 1), (HEADS, 1), 0, 4) == 0
    lighter = jax.random.randint(jax.random.fold_in(key, 2), (HEADS, 1), lowest, upper + 1)
    level = jnp.where(heavy, KMAX, lighter)
    jitter = jax.random.randint(jax.random.fold_in(key, 3), (HEADS, QBLOCKS), -1, 2)
    live = jnp.clip(level + jitter, 1, KMAX)
    chosen_head = jax.random.randint(jax.random.fold_in(key, 4), (), 0, HEADS)
    marked = (jnp.arange(HEADS)[:, None] == chosen_head) & (jnp.arange(QBLOCKS)[None, :] == 0)
    return jnp.where(marked, KMAX, live).astype(jnp.int32)


def draw_block_lists(key, part):
    noise = jax.random.randint(key, (HEADS, QBLOCKS, QBLOCKS), 0, 1 << 20)
    column = jnp.arange(QBLOCKS, dtype=jnp.int32)
    scores = noise * QBLOCKS + column[None, None, :]
    itself = column[None, :, None] == column[None, None, :]
    scores = jnp.where(itself, -1, scores)
    ranked = jnp.argsort(scores, axis=2)
    return ranked[:, :, :KMAX].astype(jnp.int32)


def steps_of(stream_key, shape, shards, least, top_value):
    loudness = 1.0
    for dim, blocks in shards:
        draws = jax.random.uniform(jax.random.fold_in(jax.random.fold_in(stream_key, 6), dim), (blocks,), jnp.float32, least / len(shards), top_value / len(shards))
        loudness = loudness * jnp.repeat(jnp.exp(draws), shape[dim] // blocks).reshape((-1,) + (1,) * (len(shape) - 1 - dim))
    return loudness


def gaussian(own_key, shape, scale, most, cuts=(), held_as=jnp.bfloat16):
    values = scale * jax.random.normal(own_key, shape, jnp.float32)
    if cuts:
        values = values * steps_of(own_key, shape, cuts, -0.22, 0.18)
    return jnp.clip(values, -most, most).astype(held_as)


def setup_inputs(seed: int = 0, part: int = 0) -> dict:
    key_list = jax.random.split(jax.random.key(seed), 11)
    own_keys = jax.random.split(jax.random.fold_in(key_list[10], part), 11)
    query_rows = draw_query_rows(jax.random.fold_in(jax.random.fold_in(key_list[10], part), 71), part)
    key_rows = draw_key_rows(jax.random.fold_in(jax.random.fold_in(key_list[10], part), 71), part)
    value_rows = gaussian(own_keys[2], (QUEUE, TOKENS, HEADS * HDIM), 1.0, 6.0, ((0, 4), (1, 4)))
    hidden_state = gaussian(own_keys[3], (QUEUE, TOKENS, D), 1.0, 6.0, ((0, 4), (1, 4)))
    modulation = gaussian(own_keys[4], (QUEUE, 2, D), 1.0, 4.0, ((0, 4),), jnp.float32)
    head_weight = gaussian(key_list[5], (D, LATENT), D ** -0.5, 0.078125)
    latents = gaussian(own_keys[6], (QUEUE, TOKENS, LATENT), 1.0, 6.0, ((0, 4), (1, 4)), jnp.float32)
    time_index = draw_time_index(jax.random.fold_in(jax.random.fold_in(key_list[10], part), 71), part)
    live_counts = draw_live_counts(jax.random.fold_in(key_list[10], 71), part)
    block_lists = draw_block_lists(jax.random.fold_in(key_list[10], 71), part)
    return dict(query_rows=query_rows, key_rows=key_rows, value_rows=value_rows, hidden_state=hidden_state, modulation=modulation, head_weight=head_weight, latents=latents, time_index=time_index, live_counts=live_counts, block_lists=block_lists)


epsilon = 1e-06
plan_shift = 5.0

def noise_level(step_value):
    fraction = step_value.astype(jnp.float32) / STEPS
    return plan_shift * fraction / (1.0 + (plan_shift - 1.0) * fraction)

def head_attention(query_head, key_head, value_head, live, blocks):
    query_blocks = query_head.astype(jnp.float32).reshape(QBLOCKS, BLK, HDIM)
    key_blocks = key_head.astype(jnp.float32).reshape(QBLOCKS, BLK, HDIM)
    value_blocks = value_head.astype(jnp.float32).reshape(QBLOCKS, BLK, HDIM)
    key_chosen = key_blocks[blocks]
    value_chosen = value_blocks[blocks]
    scores = jnp.einsum('qid,qkjd->qikj', query_blocks, key_chosen) * HDIM ** (-0.5)
    active = (jnp.arange(KMAX, dtype=jnp.int32)[None, :] < live[:, None])[:, None, :, None]
    scores = jnp.where(active, scores, -jnp.inf)
    highest = lax.optimization_barrier(jnp.max(scores, axis=(2, 3), keepdims=True))
    weights = jnp.exp(scores - highest)
    totals = lax.optimization_barrier(jnp.sum(weights, axis=(2, 3)))
    rounded = lax.optimization_barrier(weights.astype(jnp.bfloat16)).astype(jnp.float32)
    mixed = jnp.einsum('qikj,qkjd->qid', rounded, value_chosen)
    return (mixed / totals[:, :, None]).astype(jnp.bfloat16).reshape(TOKENS, HDIM)

def reference(query_rows, key_rows, value_rows, hidden_state, modulation, head_weight, latents, time_index, live_counts, block_lists):
    attended_all = []
    moved_all = []
    for position in range(QUEUE):
        query_here = query_rows[position]
        key_here = key_rows[position]
        value_here = value_rows[position]

        def per_head(head_number):
            column = (head_number * HDIM).astype(jnp.int32)
            query_head = lax.dynamic_slice_in_dim(query_here, column, HDIM, 1)
            key_head = lax.dynamic_slice_in_dim(key_here, column, HDIM, 1)
            value_head = lax.dynamic_slice_in_dim(value_here, column, HDIM, 1)
            return head_attention(query_head, key_head, value_head, live_counts[head_number], block_lists[head_number])
        stacked = lax.map(per_head, jnp.arange(HEADS, dtype=jnp.int32))
        attended_all.append(jnp.transpose(stacked, (1, 0, 2)).reshape(TOKENS, HEADS * HDIM))
        source = hidden_state[position].astype(jnp.float32)
        mean_row = lax.optimization_barrier(jnp.mean(source, axis=1, keepdims=True))
        centred = source - mean_row
        spread = lax.optimization_barrier(jnp.mean(centred * centred, axis=1, keepdims=True))
        normed = centred * lax.rsqrt(spread + epsilon)
        shaped = (normed * (1.0 + modulation[position, 1]) + modulation[position, 0]).astype(jnp.bfloat16)
        velocity = jnp.dot(shaped, head_weight, preferred_element_type=jnp.float32)
        change = noise_level(time_index[position] - 1) - noise_level(time_index[position])
        moved_all.append(latents[position] + change * velocity)
    return (jnp.stack(attended_all), jnp.roll(jnp.stack(moved_all), -1, axis=0))
```

```python
import functools

import jax
import jax.numpy as jnp
from jax import lax
from jax.experimental import pallas as pl
from jax.experimental.pallas import tpu as pltpu
from jax.sharding import PartitionSpec as P

STEPS = 8


epsilon = 1e-06
plan_shift = 5.0


def passed_along(value, axis, steps):
    count = lax.axis_size(axis)
    pairs = [(source, (source + steps) % count) for source in range(count)]
    return lax.ppermute(value, axis, pairs)


def noise_level(step_value):
    fraction = step_value.astype(jnp.float32) / STEPS
    return plan_shift * fraction / (1.0 + (plan_shift - 1.0) * fraction)


def attend(query_head, key_head, value_head, live, blocks):
    block_total = live.shape[0]
    block_size = query_head.shape[0] // block_total
    head_depth = query_head.shape[1]
    slot_total = blocks.shape[1]
    query_blocks = query_head.reshape(block_total, block_size, head_depth)
    key_blocks = key_head.reshape(-1, block_size, head_depth)
    value_blocks = value_head.reshape(-1, block_size, head_depth)
    scale = head_depth ** (-0.5)

    def advance(slot_number, state_now):
        highest, totals, summed = state_now
        chosen = lax.dynamic_index_in_dim(blocks, slot_number, 1, keepdims=False)
        key_chosen = jnp.take(key_blocks, chosen, axis=0)
        value_chosen = jnp.take(value_blocks, chosen, axis=0)
        scores = (
            jnp.einsum("bid,bjd->bij", query_blocks, key_chosen, preferred_element_type=jnp.float32)
            * scale
        )
        active = (slot_number < live)[:, None]
        new_highest = jnp.where(active, jnp.maximum(highest, jnp.max(scores, axis=2)), highest)
        weights = jnp.exp(scores - new_highest[:, :, None])
        factor = jnp.exp(highest - new_highest)
        new_totals = jnp.where(active, totals * factor + jnp.sum(weights, axis=2), totals)
        mixed = jnp.einsum(
            "bij,bjd->bid",
            weights.astype(jnp.bfloat16),
            value_chosen,
            preferred_element_type=jnp.float32,
        )
        new_summed = jnp.where(active[:, :, None], summed * factor[:, :, None] + mixed, summed)
        return (new_highest, new_totals, new_summed)

    start_state = (
        jnp.full((block_total, block_size), -jnp.inf, jnp.float32),
        jnp.zeros((block_total, block_size), jnp.float32),
        jnp.zeros((block_total, block_size, head_depth), jnp.float32),
    )
    final_state = lax.fori_loop(0, slot_total, advance, start_state)
    result = (final_state[2] / final_state[1][:, :, None]).astype(jnp.bfloat16)
    return result.reshape(block_total * block_size, head_depth)


def attend_heads(query_cols, key_cols, value_cols, head_ids, live_counts, block_lists):
    head_total = head_ids.shape[0]
    head_depth = query_cols.shape[1] // head_total
    query_stack = jnp.transpose(
        query_cols.reshape(query_cols.shape[0], head_total, head_depth), (1, 0, 2)
    )
    key_stack = jnp.transpose(
        key_cols.reshape(key_cols.shape[0], head_total, head_depth), (1, 0, 2)
    )
    value_stack = jnp.transpose(
        value_cols.reshape(value_cols.shape[0], head_total, head_depth), (1, 0, 2)
    )
    live_heads = jnp.take(live_counts, head_ids, axis=0)
    list_heads = jnp.take(block_lists, head_ids, axis=0)
    results = jax.vmap(attend)(query_stack, key_stack, value_stack, live_heads, list_heads)
    return jnp.transpose(results, (1, 0, 2)).reshape(query_cols.shape[0], head_total * head_depth)


def next_latents(hidden_state, modulation, head_weight, latents, time_index):
    source = hidden_state[0].astype(jnp.float32)
    mean_row = jnp.mean(source, axis=1, keepdims=True)
    centred = source - mean_row
    spread = jnp.mean(centred * centred, axis=1, keepdims=True)
    normed = centred * lax.rsqrt(spread + epsilon)
    shaped = (normed * (1.0 + modulation[0, 1]) + modulation[0, 0]).astype(jnp.bfloat16)
    velocity = jnp.dot(shaped, head_weight, preferred_element_type=jnp.float32)
    change = noise_level(time_index[0] - 1) - noise_level(time_index[0])
    moved = latents[0] + change * velocity
    return passed_along(moved[None].astype(jnp.bfloat16), "queue", -1).astype(jnp.float32)


def local_by_heads(
    query_rows,
    key_rows,
    value_rows,
    hidden_state,
    modulation,
    head_weight,
    latents,
    time_index,
    live_counts,
    block_lists,
):
    seq_count = lax.axis_size("seq")
    own_index = lax.axis_index("seq")
    head_count = live_counts.shape[0]
    per_device = head_count // seq_count
    order = jnp.arange(head_count, dtype=jnp.int32)
    query_send, key_send, value_send = (query_rows, key_rows, value_rows)
    query_heads, key_heads, value_heads = (
        lax.all_to_all(query_send, "seq", split_axis=2, concat_axis=1, tiled=True),
        lax.all_to_all(key_send, "seq", split_axis=2, concat_axis=1, tiled=True),
        lax.all_to_all(value_send, "seq", split_axis=2, concat_axis=1, tiled=True),
    )
    queue_next = next_latents(hidden_state, modulation, head_weight, latents, time_index)
    query_cols = query_heads[0]
    key_cols = key_heads[0]
    value_cols = value_heads[0]
    own_ids = lax.dynamic_slice_in_dim(order, own_index * per_device, per_device, 0)
    attended = attend_heads(query_cols, key_cols, value_cols, own_ids, live_counts, block_lists)
    mixed_back = lax.all_to_all(attended[None], "seq", split_axis=1, concat_axis=2, tiled=True)
    return (mixed_back, queue_next)


LEVELS = (12, 14, 16, 18, 22)
GROUP = 4


def hop_tables(live_counts, block_lists, count, me, depth):
    heads = live_counts.shape[0]
    spots = jnp.arange(count, dtype=jnp.int32)
    live = jnp.arange(block_lists.shape[2], dtype=jnp.int32)[None, None, :] < live_counts[:, :, None]
    need = jnp.any((block_lists[..., None] == spots) & live[..., None], axis=2)
    away = spots[:, None] - spots[None, :]
    reach = jnp.stack(
        [
            jnp.max(jnp.where(need, jnp.maximum(away, 0)[None], 0), axis=1),
            jnp.max(jnp.where(need, jnp.maximum(-away, 0)[None], 0), axis=1),
        ]
    ).transpose(0, 2, 1)
    numbers = jnp.arange(heads, dtype=jnp.int32)
    rank = reach * heads + (heads - 1 - numbers)
    place = jnp.sum((rank[..., None, :] > rank[..., :, None]).astype(jnp.int32), axis=-1)
    own_place = lax.dynamic_index_in_dim(place, me, 1, keepdims=False)
    order = jnp.sum(
        jnp.where(own_place[:, None, :] == numbers[None, :, None], numbers[None, None, :], 0), axis=-1
    )
    own_need = lax.dynamic_index_in_dim(need, me, 1, keepdims=False) & (spots != me)
    slot = jnp.where(own_need.T, jnp.where((spots < me)[:, None], place[0], place[1]), -1)
    used = own_need | (spots == me)
    bias = jnp.repeat(jnp.where(used, 0.0, -jnp.inf).astype(jnp.float32), depth, axis=1)
    filled = jnp.sum((lax.dynamic_index_in_dim(reach, me, 1, keepdims=False) > 0).astype(jnp.int32), axis=-1)
    most = {1: jnp.int32(0), 2: jnp.int32(0)}
    for side in range(2):
        for source in range(count):
            for hop in range(1, count):
                left = count - source - hop if side == 0 else source - hop + 1
                if left in most:
                    carried = jnp.sum((reach[side, source] >= hop).astype(jnp.int32))
                    most[left] = jnp.maximum(most[left], carried)
    return order.astype(jnp.int32), filled, slot.astype(jnp.int32), bias, most


def pack_kernel(order, filled, k_ref, v_ref, packed, sem):
    heads = packed.shape[1]
    depth = packed.shape[4]

    def copies(way, index):
        head = order[way, index]
        cols = pl.ds(pl.multiple_of(head * depth, depth), depth)
        return (
            pltpu.make_async_copy(k_ref.at[:, cols], packed.at[way, index, 0], sem.at[way, index, 0]),
            pltpu.make_async_copy(v_ref.at[:, cols], packed.at[way, index, 1], sem.at[way, index, 1]),
        )

    def begin(index, carry):
        for way in range(2):
            @pl.when(index < filled[way])
            def _():
                for copy in copies(way, index):
                    copy.start()
        return carry

    def end(index, carry):
        for way in range(2):
            @pl.when(index < filled[way])
            def _():
                for copy in copies(way, index):
                    copy.wait()
        return carry

    lax.fori_loop(0, heads, begin, 0)
    lax.fori_loop(0, heads, end, 0)


def pack_call(order, filled, key, value, heads):
    rows, width = key.shape
    depth = width // heads
    smem = pl.BlockSpec(memory_space=pltpu.SMEM)
    anywhere = pl.BlockSpec(memory_space=pl.ANY)
    return pl.pallas_call(
        pack_kernel,
        out_shape=jax.ShapeDtypeStruct((2, heads, 2, rows, depth), key.dtype),
        in_specs=[smem, smem, anywhere, anywhere],
        out_specs=anywhere,
        scratch_shapes=[pltpu.SemaphoreType.DMA((2, heads, 2))],
    )(order, filled, key, value)


def hop_kernel(level, count, packed, arrived, send_sem, recv_sem):
    ways = 2
    heads = packed.shape[1]
    me = lax.axis_index("seq")
    caps = (0, level, min(heads, level * 3 // 2), heads)

    def cap(dests):
        value = jnp.int32(0)
        for number in range(1, count):
            value = jnp.where(dests == number, min(caps[number], heads), value)
        return value

    incoming = (cap(count - me), cap(me + 1))
    outgoing = (cap(count - 1 - me), cap(me))
    targets = (me + 1, me - 1)
    has_target = (me < count - 1, me > 0)

    def source_exists(way, hop):
        return me >= hop if way == 0 else me + hop < count

    def hop_copy(way, hop, index, source):
        origin = packed.at[way, index] if hop == 1 else arrived.at[source, index]
        return pltpu.make_async_remote_copy(
            src_ref=origin,
            dst_ref=arrived.at[source, index],
            send_sem=send_sem.at[way, hop - 1, index],
            recv_sem=recv_sem.at[way, hop - 1, index],
            device_id={"seq": targets[way]},
            device_id_type=pl.DeviceIdType.MESH,
        )

    def back(way, hops):
        return me - hops if way == 0 else me + hops

    barrier = pltpu.get_barrier_semaphore()
    for way in range(ways):
        @pl.when(has_target[way])
        def _():
            pl.semaphore_signal(
                barrier, inc=1, device_id={"seq": targets[way]}, device_id_type=pl.DeviceIdType.MESH
            )
    pl.semaphore_wait(barrier, jnp.where((me == 0) | (me == count - 1), 1, 2))

    def launch(index, carry):
        for way in range(ways):
            @pl.when(index < outgoing[way])
            def _():
                hop_copy(way, 1, index, me).start()
        return carry

    lax.fori_loop(0, jnp.maximum(outgoing[0], outgoing[1]), launch, 0)

    for hop in range(1, count):
        def pass_on(index, carry):
            for way in range(ways):
                @pl.when(source_exists(way, hop) & (index < incoming[way]))
                def _():
                    hop_copy(way, hop, index, back(way, hop)).wait_recv()
                if hop < count - 1:
                    @pl.when(source_exists(way, hop) & (index < outgoing[way]))
                    def _():
                        hop_copy(way, hop + 1, index, back(way, hop)).start()
            return carry

        lax.fori_loop(0, jnp.maximum(incoming[0], incoming[1]), pass_on, 0)

    for hop in range(1, count):
        def drain(index, carry):
            for way in range(ways):
                sends = index < outgoing[way]
                if hop > 1:
                    sends = sends & source_exists(way, hop - 1)

                @pl.when(sends)
                def _():
                    hop_copy(way, hop, index, back(way, hop - 1)).wait_send()
            return carry

        lax.fori_loop(0, jnp.maximum(outgoing[0], outgoing[1]), drain, 0)


def hop_call(level, collective, count, packed):
    _, heads, _, rows, depth = packed.shape
    anywhere = pl.BlockSpec(memory_space=pl.ANY)
    return pl.pallas_call(
        functools.partial(hop_kernel, level, count),
        out_shape=jax.ShapeDtypeStruct((count, heads, 2, rows, depth), packed.dtype),
        in_specs=[anywhere],
        out_specs=anywhere,
        scratch_shapes=[
            pltpu.SemaphoreType.DMA((2, count - 1, heads)),
            pltpu.SemaphoreType.DMA((2, count - 1, heads)),
        ],
        compiler_params=pltpu.CompilerParams(collective_id=collective, has_side_effects=True),
    )(packed)


def attend_kernel(slot, bias, q_ref, k_ref, v_ref, arrived, out_ref, held, sem):
    heads, _, count, rows, depth = held.shape
    me = lax.axis_index("seq")

    def columns(head):
        return pl.ds(pl.multiple_of(head * depth, depth), depth)

    def own_copies(head):
        return (
            pltpu.make_async_copy(k_ref.at[:, columns(head)], held.at[head, 0, me], sem.at[head, me]),
            pltpu.make_async_copy(v_ref.at[:, columns(head)], held.at[head, 1, me], sem.at[head, count]),
        )

    def far_copy(head, source):
        return pltpu.make_async_copy(
            arrived.at[source, slot[source, head]], held.at[head, :, source], sem.at[head, source]
        )

    def fetch(head, carry):
        for copy in own_copies(head):
            copy.start()
        for source in range(count):
            @pl.when(slot[source, head] >= 0)
            def _():
                far_copy(head, source).start()

            @pl.when((slot[source, head] < 0) & (source != me))
            def _():
                held[head, :, source] = jnp.zeros((2, rows, depth), held.dtype)
        return carry

    lax.fori_loop(0, heads, fetch, 0)
    scale = depth ** (-0.5)

    def attend(step, carry):
        results = []
        for offset in range(GROUP):
            head = step * GROUP + offset
            for copy in own_copies(head):
                copy.wait()
            for source in range(count):
                @pl.when(slot[source, head] >= 0)
                def _():
                    far_copy(head, source).wait()
        for offset in range(GROUP):
            head = step * GROUP + offset
            scores = scale * lax.dot_general(
                q_ref[:, columns(head)], held[head, 0].reshape(count * rows, depth),
                (((1,), (1,)), ((), ())), preferred_element_type=jnp.float32,
            ) + bias[pl.ds(head, 1), :]
            weights = jnp.exp(scores - jnp.max(scores, axis=1, keepdims=True))
            mixed = jnp.dot(
                weights.astype(jnp.bfloat16), held[head, 1].reshape(count * rows, depth),
                preferred_element_type=jnp.float32,
            )
            results.append((head, (mixed / jnp.sum(weights, axis=1, keepdims=True)).astype(jnp.bfloat16)))
        for head, value in results:
            out_ref[:, columns(head)] = value
        return carry

    lax.fori_loop(0, heads // GROUP, attend, 0)


def attend_call(slot, bias, query, key, value, arrived):
    count, heads, _, rows, depth = arrived.shape
    smem = pl.BlockSpec(memory_space=pltpu.SMEM)
    vmem = pl.BlockSpec(memory_space=pltpu.VMEM)
    anywhere = pl.BlockSpec(memory_space=pl.ANY)
    return pl.pallas_call(
        attend_kernel,
        out_shape=jax.ShapeDtypeStruct(query.shape, jnp.bfloat16),
        in_specs=[smem, vmem, vmem, anywhere, anywhere, anywhere],
        out_specs=vmem,
        scratch_shapes=[
            pltpu.VMEM((heads, 2, count, rows, depth), jnp.bfloat16),
            pltpu.SemaphoreType.DMA((heads, count + 1)),
        ],
        compiler_params=pltpu.CompilerParams(vmem_limit_bytes=40 * 1024 * 1024),
    )(slot, bias, query, key, value, arrived)


def local_by_blocks(
    query_rows,
    key_rows,
    value_rows,
    hidden_state,
    modulation,
    head_weight,
    latents,
    time_index,
    live_counts,
    block_lists,
):
    count = lax.axis_size("seq")
    me = lax.axis_index("seq")
    heads = live_counts.shape[0]
    depth = query_rows.shape[2] // heads
    order, filled, slot, bias, most = hop_tables(live_counts, block_lists, count, me, depth)
    levels = tuple(level for level in LEVELS if level < heads) + (heads,)
    chosen = jnp.int32(0)
    for level in levels[:-1]:
        over = (most[1] > level) | (most[2] > level * 3 // 2)
        chosen = chosen + over.astype(jnp.int32)
    calls = [
        functools.partial(hop_call, level, number, count) for number, level in enumerate(levels)
    ]
    queue_next = next_latents(hidden_state, modulation, head_weight, latents, time_index)
    packed = pack_call(order, filled, key_rows[0], value_rows[0], heads)
    arrived = lax.switch(chosen, calls, packed)
    attended = attend_call(slot, bias, query_rows[0], key_rows[0], value_rows[0], arrived)
    return (attended[None], queue_next)


def solution(mesh):
    seq_count = mesh.shape["seq"]

    def local(*arrays):
        blocks = arrays[8].shape[1]
        fits = seq_count <= 4 and blocks == seq_count and arrays[0].shape[1] == arrays[0].shape[2] // arrays[8].shape[0]
        return (local_by_blocks if fits else local_by_heads)(*arrays)

    placed = (
        P(("groups", "queue"), "seq", None),
        P(("groups", "queue"), "seq", None),
        P(("groups", "queue"), "seq", None),
        P(("groups", "queue"), "seq", None),
        P(("groups", "queue"), None, None),
        P(),
        P(("groups", "queue"), "seq", None),
        P(("groups", "queue")),
        P(),
        P(),
    )
    return jax.shard_map(
        local,
        mesh=mesh,
        in_specs=placed,
        out_specs=(P(("groups", "queue"), "seq", None), P(("groups", "queue"), "seq", None)),
        check_vma=False,
    )
```

```python
import functools

import jax
import jax.numpy as jnp
from jax import lax
from jax.experimental import pallas as pl
from jax.experimental.pallas import tpu as pltpu
from jax.sharding import PartitionSpec as P

STEPS = 8


epsilon = 1e-06
plan_shift = 5.0


def passed_along(value, axis, steps):
    count = lax.axis_size(axis)
    pairs = [(source, (source + steps) % count) for source in range(count)]
    return lax.ppermute(value, axis, pairs)


def noise_level(step_value):
    fraction = step_value.astype(jnp.float32) / STEPS
    return plan_shift * fraction / (1.0 + (plan_shift - 1.0) * fraction)


def attend(query_head, key_head, value_head, live, blocks):
    block_total = live.shape[0]
    block_size = query_head.shape[0] // block_total
    head_depth = query_head.shape[1]
    slot_total = blocks.shape[1]
    query_blocks = query_head.reshape(block_total, block_size, head_depth)
    key_blocks = key_head.reshape(-1, block_size, head_depth)
    value_blocks = value_head.reshape(-1, block_size, head_depth)
    scale = head_depth ** (-0.5)

    def advance(slot_number, state_now):
        highest, totals, summed = state_now
        chosen = lax.dynamic_index_in_dim(blocks, slot_number, 1, keepdims=False)
        key_chosen = jnp.take(key_blocks, chosen, axis=0)
        value_chosen = jnp.take(value_blocks, chosen, axis=0)
        scores = (
            jnp.einsum("bid,bjd->bij", query_blocks, key_chosen, preferred_element_type=jnp.float32)
            * scale
        )
        active = (slot_number < live)[:, None]
        new_highest = jnp.where(active, jnp.maximum(highest, jnp.max(scores, axis=2)), highest)
        weights = jnp.exp(scores - new_highest[:, :, None])
        factor = jnp.exp(highest - new_highest)
        new_totals = jnp.where(active, totals * factor + jnp.sum(weights, axis=2), totals)
        mixed = jnp.einsum(
            "bij,bjd->bid",
            weights.astype(jnp.bfloat16),
            value_chosen,
            preferred_element_type=jnp.float32,
        )
        new_summed = jnp.where(active[:, :, None], summed * factor[:, :, None] + mixed, summed)
        return (new_highest, new_totals, new_summed)

    start_state = (
        jnp.full((block_total, block_size), -jnp.inf, jnp.float32),
        jnp.zeros((block_total, block_size), jnp.float32),
        jnp.zeros((block_total, block_size, head_depth), jnp.float32),
    )
    final_state = lax.fori_loop(0, slot_total, advance, start_state)
    result = (final_state[2] / final_state[1][:, :, None]).astype(jnp.bfloat16)
    return result.reshape(block_total * block_size, head_depth)


def attend_heads(query_cols, key_cols, value_cols, head_ids, live_counts, block_lists):
    head_total = head_ids.shape[0]
    head_depth = query_cols.shape[1] // head_total
    query_stack = jnp.transpose(
        query_cols.reshape(query_cols.shape[0], head_total, head_depth), (1, 0, 2)
    )
    key_stack = jnp.transpose(
        key_cols.reshape(key_cols.shape[0], head_total, head_depth), (1, 0, 2)
    )
    value_stack = jnp.transpose(
        value_cols.reshape(value_cols.shape[0], head_total, head_depth), (1, 0, 2)
    )
    live_heads = jnp.take(live_counts, head_ids, axis=0)
    list_heads = jnp.take(block_lists, head_ids, axis=0)
    results = jax.vmap(attend)(query_stack, key_stack, value_stack, live_heads, list_heads)
    return jnp.transpose(results, (1, 0, 2)).reshape(query_cols.shape[0], head_total * head_depth)


def next_latents(hidden_state, modulation, head_weight, latents, time_index):
    source = hidden_state[0].astype(jnp.float32)
    mean_row = jnp.mean(source, axis=1, keepdims=True)
    centred = source - mean_row
    spread = jnp.mean(centred * centred, axis=1, keepdims=True)
    normed = centred * lax.rsqrt(spread + epsilon)
    shaped = (normed * (1.0 + modulation[0, 1]) + modulation[0, 0]).astype(jnp.bfloat16)
    velocity = jnp.dot(shaped, head_weight, preferred_element_type=jnp.float32)
    change = noise_level(time_index[0] - 1) - noise_level(time_index[0])
    moved = latents[0] + change * velocity
    return passed_along(moved[None].astype(jnp.bfloat16), "queue", -1).astype(jnp.float32)


def local_by_heads(
    query_rows,
    key_rows,
    value_rows,
    hidden_state,
    modulation,
    head_weight,
    latents,
    time_index,
    live_counts,
    block_lists,
):
    seq_count = lax.axis_size("seq")
    own_index = lax.axis_index("seq")
    head_count = live_counts.shape[0]
    per_device = head_count // seq_count
    order = jnp.arange(head_count, dtype=jnp.int32)
    query_send, key_send, value_send = (query_rows, key_rows, value_rows)
    query_heads, key_heads, value_heads = (
        lax.all_to_all(query_send, "seq", split_axis=2, concat_axis=1, tiled=True),
        lax.all_to_all(key_send, "seq", split_axis=2, concat_axis=1, tiled=True),
        lax.all_to_all(value_send, "seq", split_axis=2, concat_axis=1, tiled=True),
    )
    queue_next = next_latents(hidden_state, modulation, head_weight, latents, time_index)
    query_cols = query_heads[0]
    key_cols = key_heads[0]
    value_cols = value_heads[0]
    own_ids = lax.dynamic_slice_in_dim(order, own_index * per_device, per_device, 0)
    attended = attend_heads(query_cols, key_cols, value_cols, own_ids, live_counts, block_lists)
    mixed_back = lax.all_to_all(attended[None], "seq", split_axis=1, concat_axis=2, tiled=True)
    return (mixed_back, queue_next)


LEVELS = (12, 13, 14, 15, 16, 17, 18, 21)
GROUP = 4
ROWS = 16


def hop_tables(live_counts, block_lists, count, me):
    heads = live_counts.shape[0]
    spots = jnp.arange(count, dtype=jnp.int32)
    live = jnp.arange(block_lists.shape[2], dtype=jnp.int32)[None, None, :] < live_counts[:, :, None]
    need = jnp.any((block_lists[..., None] == spots) & live[..., None], axis=2)
    away = spots[:, None] - spots[None, :]
    reach = jnp.stack(
        [
            jnp.max(jnp.where(need, jnp.maximum(away, 0)[None], 0), axis=1),
            jnp.max(jnp.where(need, jnp.maximum(-away, 0)[None], 0), axis=1),
        ]
    ).transpose(0, 2, 1)
    numbers = jnp.arange(heads, dtype=jnp.int32)
    rank = reach * heads + (heads - 1 - numbers)
    place = jnp.sum((rank[..., None, :] > rank[..., :, None]).astype(jnp.int32), axis=-1)
    own_place = lax.dynamic_index_in_dim(place, me, 1, keepdims=False)
    order = jnp.sum(
        jnp.where(own_place[:, None, :] == numbers[None, :, None], numbers[None, None, :], 0), axis=-1
    )
    own_need = lax.dynamic_index_in_dim(need, me, 1, keepdims=False) & (spots != me)
    slot = jnp.where(own_need.T, jnp.where((spots < me)[:, None], place[0], place[1]), 0)
    bias = jnp.where(own_need.T, 0.0, -jnp.inf).astype(jnp.float32)
    filled = jnp.sum((lax.dynamic_index_in_dim(reach, me, 1, keepdims=False) > 0).astype(jnp.int32), axis=-1)
    most = {1: jnp.int32(0), 2: jnp.int32(0)}
    for side in range(2):
        for source in range(count):
            for hop in range(1, count):
                left = count - source - hop if side == 0 else source - hop + 1
                if left in most:
                    carried = jnp.sum((reach[side, source] >= hop).astype(jnp.int32))
                    most[left] = jnp.maximum(most[left], carried)
    return order.astype(jnp.int32), filled, slot.astype(jnp.int32), bias, most


def pack_kernel(order, filled, k_ref, v_ref, packed, staged, sem):
    _, heads, _, rows, depth = packed.shape

    def copy(way, index):
        return pltpu.make_async_copy(staged.at[way, index], packed.at[way, index], sem.at[way, index])

    def begin(index, carry):
        for way in range(2):
            @pl.when(index < jnp.maximum(filled[way], 1))
            def _():
                head = order[way, index]
                cols = pl.ds(pl.multiple_of(head * depth, depth), depth)
                staged[way, index, 0] = k_ref[:, cols]
                staged[way, index, 1] = v_ref[:, cols]
                copy(way, index).start()
        return carry

    def end(index, carry):
        for way in range(2):
            @pl.when(index < jnp.maximum(filled[way], 1))
            def _():
                copy(way, index).wait()
        return carry

    lax.fori_loop(0, heads, begin, 0)
    lax.fori_loop(0, heads, end, 0)


def pack_call(order, filled, key, value, heads):
    rows, width = key.shape
    depth = width // heads
    smem = pl.BlockSpec(memory_space=pltpu.SMEM)
    vmem = pl.BlockSpec(memory_space=pltpu.VMEM)
    return pl.pallas_call(
        pack_kernel,
        out_shape=jax.ShapeDtypeStruct((2, heads, 2, rows, depth), key.dtype),
        in_specs=[smem, smem, vmem, vmem],
        out_specs=pl.BlockSpec(memory_space=pl.ANY),
        scratch_shapes=[
            pltpu.VMEM((2, heads, 2, rows, depth), key.dtype),
            pltpu.SemaphoreType.DMA((2, heads)),
        ],
        compiler_params=pltpu.CompilerParams(vmem_limit_bytes=24 * 1024 * 1024),
    )(order, filled, key, value)


def hop_kernel(
    level, count, packed, time_ref, hidden, modulation, weight, latents, arrived, moved, shaped, send_sem, recv_sem
):
    ways = 2
    heads = packed.shape[1]
    me = lax.axis_index("seq")
    caps = (0, level, min(heads, level * 3 // 2), heads)

    def cap(dests):
        value = jnp.int32(0)
        for number in range(1, count):
            value = jnp.where(dests == number, min(caps[number], heads), value)
        return value

    incoming = (cap(count - me), cap(me + 1))
    outgoing = (cap(count - 1 - me), cap(me))
    targets = (me + 1, me - 1)
    has_target = (me < count - 1, me > 0)

    def source_exists(way, hop):
        return me >= hop if way == 0 else me + hop < count

    def hop_copy(way, hop, index, source):
        origin = packed.at[way, index] if hop == 1 else arrived.at[source, index]
        return pltpu.make_async_remote_copy(
            src_ref=origin,
            dst_ref=arrived.at[source, index],
            send_sem=send_sem.at[way, hop - 1, index],
            recv_sem=recv_sem.at[way, hop - 1, index],
            device_id={"seq": targets[way]},
            device_id_type=pl.DeviceIdType.MESH,
        )

    def back(way, hops):
        return me - hops if way == 0 else me + hops

    barrier = pltpu.get_barrier_semaphore()
    for way in range(ways):
        @pl.when(has_target[way])
        def _():
            pl.semaphore_signal(
                barrier, inc=1, device_id={"seq": targets[way]}, device_id_type=pl.DeviceIdType.MESH
            )
    pl.semaphore_wait(barrier, jnp.where((me == 0) | (me == count - 1), 1, 2))

    def launch(index, carry):
        for way in range(ways):
            @pl.when(index < outgoing[way])
            def _():
                hop_copy(way, 1, index, me).start()
        return carry

    lax.fori_loop(0, jnp.maximum(outgoing[0], outgoing[1]), launch, 0)

    def shape_rows(step, carry):
        part = pl.ds(pl.multiple_of(step * ROWS, ROWS), ROWS)
        source = hidden[part, :].astype(jnp.float32)
        centred = source - jnp.mean(source, axis=1, keepdims=True)
        spread = jnp.mean(centred * centred, axis=1, keepdims=True)
        normed = centred * lax.rsqrt(spread + epsilon)
        shaped[part, :] = (normed * (1.0 + modulation[1:2, :]) + modulation[0:1, :]).astype(jnp.bfloat16)
        return carry

    lax.fori_loop(0, hidden.shape[0] // ROWS, shape_rows, 0)
    velocity = jnp.dot(shaped[...], weight[...], preferred_element_type=jnp.float32)
    now = jnp.full((1, latents.shape[1]), time_ref[0], jnp.int32)
    change = noise_level(now - 1) - noise_level(now)
    moved[...] = (latents[...] + change * velocity).astype(jnp.bfloat16)

    for hop in range(1, count):
        def pass_on(index, carry):
            for way in range(ways):
                @pl.when(source_exists(way, hop) & (index < incoming[way]))
                def _():
                    hop_copy(way, hop, index, back(way, hop)).wait_recv()
                if hop < count - 1:
                    @pl.when(source_exists(way, hop) & (index < outgoing[way]))
                    def _():
                        hop_copy(way, hop + 1, index, back(way, hop)).start()
            return carry

        lax.fori_loop(0, jnp.maximum(incoming[0], incoming[1]), pass_on, 0)

    for hop in range(1, count):
        def drain(index, carry):
            for way in range(ways):
                sends = index < outgoing[way]
                if hop > 1:
                    sends = sends & source_exists(way, hop - 1)

                @pl.when(sends)
                def _():
                    hop_copy(way, hop, index, back(way, hop - 1)).wait_send()
            return carry

        lax.fori_loop(0, jnp.maximum(outgoing[0], outgoing[1]), drain, 0)


def hop_call(level, collective, count, packed, time_index, hidden, modulation, weight, latents):
    _, heads, _, rows, depth = packed.shape
    anywhere = pl.BlockSpec(memory_space=pl.ANY)
    vmem = pl.BlockSpec(memory_space=pltpu.VMEM)
    return pl.pallas_call(
        functools.partial(hop_kernel, level, count),
        out_shape=(
            jax.ShapeDtypeStruct((count, heads, 2, rows, depth), packed.dtype),
            jax.ShapeDtypeStruct(latents.shape, jnp.bfloat16),
        ),
        in_specs=[anywhere, pl.BlockSpec(memory_space=pltpu.SMEM), vmem, vmem, vmem, vmem],
        out_specs=(anywhere, vmem),
        scratch_shapes=[
            pltpu.VMEM(hidden.shape, jnp.bfloat16),
            pltpu.SemaphoreType.DMA((2, count - 1, heads)),
            pltpu.SemaphoreType.DMA((2, count - 1, heads)),
        ],
        compiler_params=pltpu.CompilerParams(
            collective_id=collective, has_side_effects=True, vmem_limit_bytes=24 * 1024 * 1024
        ),
    )(packed, time_index, hidden, modulation, weight, latents)


def attend_kernel(slot, bias, q_ref, k_ref, v_ref, arrived, out_ref):
    count, heads, _, rows, depth = arrived.shape
    me = lax.axis_index("seq")
    scale = depth ** (-0.5)

    def attend(step, carry):
        results = []
        for offset in range(GROUP):
            head = step * GROUP + offset
            cols = pl.ds(pl.multiple_of(head * depth, depth), depth)
            query = q_ref[:, cols]
            keys, values, adds = [k_ref[:, cols]], [v_ref[:, cols]], [jnp.float32(0)]
            for step_away in range(1, count):
                source = lax.rem(me + step_away, count)
                keys.append(arrived[source, slot[source, head], 0])
                values.append(arrived[source, slot[source, head], 1])
                adds.append(bias[source, head])
            scores = [
                scale * lax.dot_general(
                    query, one, (((1,), (1,)), ((), ())), preferred_element_type=jnp.float32
                ) + add
                for one, add in zip(keys, adds)
            ]
            top = jnp.max(functools.reduce(jnp.maximum, scores), axis=1, keepdims=True)
            weights = [jnp.exp(one - top) for one in scores]
            part = jnp.sum(sum(weights), axis=1, keepdims=True)
            mixed = jnp.dot(
                jnp.concatenate([one.astype(jnp.bfloat16) for one in weights], axis=1),
                jnp.concatenate(values, axis=0),
                preferred_element_type=jnp.float32,
            )
            results.append((cols, (mixed / part).astype(jnp.bfloat16)))
        for cols, value in results:
            out_ref[:, cols] = value
        return carry

    lax.fori_loop(0, heads // GROUP, attend, 0)


def attend_call(slot, bias, query, key, value, arrived):
    rows, width = query.shape
    count = arrived.shape[0]
    smem = pl.BlockSpec(memory_space=pltpu.SMEM)
    vmem = pl.BlockSpec(memory_space=pltpu.VMEM)
    return pl.pallas_call(
        attend_kernel,
        out_shape=jax.ShapeDtypeStruct(query.shape, jnp.bfloat16),
        in_specs=[smem, smem, vmem, vmem, vmem, vmem],
        out_specs=vmem,
        compiler_params=pltpu.CompilerParams(vmem_limit_bytes=32 * 1024 * 1024),
        cost_estimate=pl.CostEstimate(
            flops=4 * count * rows * rows * width,
            bytes_accessed=8 * rows * width + 4 * count * rows * width,
            transcendentals=count * rows * width,
        ),
    )(slot, bias, query, key, value, arrived)


def local_by_blocks(
    query_rows,
    key_rows,
    value_rows,
    hidden_state,
    modulation,
    head_weight,
    latents,
    time_index,
    live_counts,
    block_lists,
):
    count = lax.axis_size("seq")
    me = lax.axis_index("seq")
    heads = live_counts.shape[0]
    order, filled, slot, bias, most = hop_tables(live_counts, block_lists, count, me)
    levels = tuple(level for level in LEVELS if level < heads) + (heads,)
    chosen = jnp.int32(0)
    for level in levels[:-1]:
        over = (most[1] > level) | (most[2] > level * 3 // 2)
        chosen = chosen + over.astype(jnp.int32)
    calls = [
        functools.partial(hop_call, level, number, count) for number, level in enumerate(levels)
    ]
    packed = pack_call(order, filled, key_rows[0], value_rows[0], heads)
    arrived, moved = lax.switch(
        chosen, calls, packed, time_index, hidden_state[0], modulation[0], head_weight, latents[0]
    )
    queue_next = passed_along(moved[None], "queue", -1).astype(jnp.float32)
    attended = attend_call(slot, bias, query_rows[0], key_rows[0], value_rows[0], arrived)
    return (attended[None], queue_next)


def solution(mesh):
    seq_count = mesh.shape["seq"]

    def local(*arrays):
        blocks = arrays[8].shape[1]
        fits = seq_count <= 4 and blocks == seq_count and arrays[0].shape[1] == arrays[0].shape[2] // arrays[8].shape[0]
        return (local_by_blocks if fits else local_by_heads)(*arrays)

    placed = (
        P(("groups", "queue"), "seq", None),
        P(("groups", "queue"), "seq", None),
        P(("groups", "queue"), "seq", None),
        P(("groups", "queue"), "seq", None),
        P(("groups", "queue"), None, None),
        P(),
        P(("groups", "queue"), "seq", None),
        P(("groups", "queue")),
        P(),
        P(),
    )
    return jax.shard_map(
        local,
        mesh=mesh,
        in_specs=placed,
        out_specs=(P(("groups", "queue"), "seq", None), P(("groups", "queue"), "seq", None)),
        check_vma=False,
    )
```

```python
import functools

import jax
import jax.numpy as jnp
from jax import lax
from jax.experimental import pallas as pl
from jax.experimental.pallas import tpu as pltpu
from jax.sharding import PartitionSpec as P

STEPS = 8


epsilon = 1e-06
plan_shift = 5.0


def passed_along(value, axis, steps):
    count = lax.axis_size(axis)
    pairs = [(source, (source + steps) % count) for source in range(count)]
    return lax.ppermute(value, axis, pairs)


def noise_level(step_value):
    fraction = step_value.astype(jnp.float32) / STEPS
    return plan_shift * fraction / (1.0 + (plan_shift - 1.0) * fraction)


def attend(query_head, key_head, value_head, live, blocks):
    block_total = live.shape[0]
    block_size = query_head.shape[0] // block_total
    head_depth = query_head.shape[1]
    slot_total = blocks.shape[1]
    query_blocks = query_head.reshape(block_total, block_size, head_depth)
    key_blocks = key_head.reshape(-1, block_size, head_depth)
    value_blocks = value_head.reshape(-1, block_size, head_depth)
    scale = head_depth ** (-0.5)

    def advance(slot_number, state_now):
        highest, totals, summed = state_now
        chosen = lax.dynamic_index_in_dim(blocks, slot_number, 1, keepdims=False)
        key_chosen = jnp.take(key_blocks, chosen, axis=0)
        value_chosen = jnp.take(value_blocks, chosen, axis=0)
        scores = (
            jnp.einsum("bid,bjd->bij", query_blocks, key_chosen, preferred_element_type=jnp.float32)
            * scale
        )
        active = (slot_number < live)[:, None]
        new_highest = jnp.where(active, jnp.maximum(highest, jnp.max(scores, axis=2)), highest)
        weights = jnp.exp(scores - new_highest[:, :, None])
        factor = jnp.exp(highest - new_highest)
        new_totals = jnp.where(active, totals * factor + jnp.sum(weights, axis=2), totals)
        mixed = jnp.einsum(
            "bij,bjd->bid",
            weights.astype(jnp.bfloat16),
            value_chosen,
            preferred_element_type=jnp.float32,
        )
        new_summed = jnp.where(active[:, :, None], summed * factor[:, :, None] + mixed, summed)
        return (new_highest, new_totals, new_summed)

    start_state = (
        jnp.full((block_total, block_size), -jnp.inf, jnp.float32),
        jnp.zeros((block_total, block_size), jnp.float32),
        jnp.zeros((block_total, block_size, head_depth), jnp.float32),
    )
    final_state = lax.fori_loop(0, slot_total, advance, start_state)
    result = (final_state[2] / final_state[1][:, :, None]).astype(jnp.bfloat16)
    return result.reshape(block_total * block_size, head_depth)


def attend_heads(query_cols, key_cols, value_cols, head_ids, live_counts, block_lists):
    head_total = head_ids.shape[0]
    head_depth = query_cols.shape[1] // head_total
    query_stack = jnp.transpose(
        query_cols.reshape(query_cols.shape[0], head_total, head_depth), (1, 0, 2)
    )
    key_stack = jnp.transpose(
        key_cols.reshape(key_cols.shape[0], head_total, head_depth), (1, 0, 2)
    )
    value_stack = jnp.transpose(
        value_cols.reshape(value_cols.shape[0], head_total, head_depth), (1, 0, 2)
    )
    live_heads = jnp.take(live_counts, head_ids, axis=0)
    list_heads = jnp.take(block_lists, head_ids, axis=0)
    results = jax.vmap(attend)(query_stack, key_stack, value_stack, live_heads, list_heads)
    return jnp.transpose(results, (1, 0, 2)).reshape(query_cols.shape[0], head_total * head_depth)


def next_latents(hidden_state, modulation, head_weight, latents, time_index):
    source = hidden_state[0].astype(jnp.float32)
    mean_row = jnp.mean(source, axis=1, keepdims=True)
    centred = source - mean_row
    spread = jnp.mean(centred * centred, axis=1, keepdims=True)
    normed = centred * lax.rsqrt(spread + epsilon)
    shaped = (normed * (1.0 + modulation[0, 1]) + modulation[0, 0]).astype(jnp.bfloat16)
    velocity = jnp.dot(shaped, head_weight, preferred_element_type=jnp.float32)
    change = noise_level(time_index[0] - 1) - noise_level(time_index[0])
    moved = latents[0] + change * velocity
    return passed_along(moved[None].astype(jnp.bfloat16), "queue", -1).astype(jnp.float32)


def local_by_heads(
    query_rows,
    key_rows,
    value_rows,
    hidden_state,
    modulation,
    head_weight,
    latents,
    time_index,
    live_counts,
    block_lists,
):
    seq_count = lax.axis_size("seq")
    own_index = lax.axis_index("seq")
    head_count = live_counts.shape[0]
    per_device = head_count // seq_count
    order = jnp.arange(head_count, dtype=jnp.int32)
    query_send, key_send, value_send = (query_rows, key_rows, value_rows)
    query_heads, key_heads, value_heads = (
        lax.all_to_all(query_send, "seq", split_axis=2, concat_axis=1, tiled=True),
        lax.all_to_all(key_send, "seq", split_axis=2, concat_axis=1, tiled=True),
        lax.all_to_all(value_send, "seq", split_axis=2, concat_axis=1, tiled=True),
    )
    queue_next = next_latents(hidden_state, modulation, head_weight, latents, time_index)
    query_cols = query_heads[0]
    key_cols = key_heads[0]
    value_cols = value_heads[0]
    own_ids = lax.dynamic_slice_in_dim(order, own_index * per_device, per_device, 0)
    attended = attend_heads(query_cols, key_cols, value_cols, own_ids, live_counts, block_lists)
    mixed_back = lax.all_to_all(attended[None], "seq", split_axis=1, concat_axis=2, tiled=True)
    return (mixed_back, queue_next)


LEVELS = (12, 13, 14, 15, 16, 17, 18, 21)
GROUP = 4
ROWS = 16


def hop_tables(live_counts, block_lists, count, me):
    heads = live_counts.shape[0]
    spots = jnp.arange(count, dtype=jnp.int32)
    live = jnp.arange(block_lists.shape[2], dtype=jnp.int32)[None, None, :] < live_counts[:, :, None]
    need = jnp.any((block_lists[..., None] == spots) & live[..., None], axis=2)
    away = spots[:, None] - spots[None, :]
    reach = jnp.stack(
        [
            jnp.max(jnp.where(need, jnp.maximum(away, 0)[None], 0), axis=1),
            jnp.max(jnp.where(need, jnp.maximum(-away, 0)[None], 0), axis=1),
        ]
    ).transpose(0, 2, 1)
    numbers = jnp.arange(heads, dtype=jnp.int32)
    rank = reach * heads + (heads - 1 - numbers)
    place = jnp.sum((rank[..., None, :] > rank[..., :, None]).astype(jnp.int32), axis=-1)
    own_place = lax.dynamic_index_in_dim(place, me, 1, keepdims=False)
    order = jnp.sum(
        jnp.where(own_place[:, None, :] == numbers[None, :, None], numbers[None, None, :], 0), axis=-1
    )
    own_need = lax.dynamic_index_in_dim(need, me, 1, keepdims=False) & (spots != me)
    slot = jnp.where(own_need.T, jnp.where((spots < me)[:, None], place[0], place[1]), 0)
    bias = jnp.where(own_need.T, 0.0, -jnp.inf).astype(jnp.float32)
    filled = jnp.sum((lax.dynamic_index_in_dim(reach, me, 1, keepdims=False) > 0).astype(jnp.int32), axis=-1)
    most = {1: jnp.int32(0), 2: jnp.int32(0), 3: jnp.int32(0)}
    for side in range(2):
        for source in range(count):
            for hop in range(1, count):
                left = count - source - hop if side == 0 else source - hop + 1
                if left in most:
                    carried = jnp.sum((reach[side, source] >= hop).astype(jnp.int32))
                    most[left] = jnp.maximum(most[left], carried)
    return order.astype(jnp.int32), filled, slot.astype(jnp.int32), bias, most


def pack_kernel(order, filled, k_ref, v_ref, packed, staged, sem):
    _, heads, _, rows, depth = packed.shape

    def copy(way, index):
        return pltpu.make_async_copy(staged.at[way, index], packed.at[way, index], sem.at[way, index])

    def begin(index, carry):
        for way in range(2):
            @pl.when(index < jnp.maximum(filled[way], 1))
            def _():
                head = order[way, index]
                cols = pl.ds(pl.multiple_of(head * depth, depth), depth)
                staged[way, index, 0] = k_ref[:, cols]
                staged[way, index, 1] = v_ref[:, cols]
                copy(way, index).start()
        return carry

    def end(index, carry):
        for way in range(2):
            @pl.when(index < jnp.maximum(filled[way], 1))
            def _():
                copy(way, index).wait()
        return carry

    lax.fori_loop(0, heads, begin, 0)
    lax.fori_loop(0, heads, end, 0)


def pack_call(order, filled, key, value, heads):
    rows, width = key.shape
    depth = width // heads
    smem = pl.BlockSpec(memory_space=pltpu.SMEM)
    vmem = pl.BlockSpec(memory_space=pltpu.VMEM)
    return pl.pallas_call(
        pack_kernel,
        out_shape=jax.ShapeDtypeStruct((2, heads, 2, rows, depth), key.dtype),
        in_specs=[smem, smem, vmem, vmem],
        out_specs=pl.BlockSpec(memory_space=pl.ANY),
        scratch_shapes=[
            pltpu.VMEM((2, heads, 2, rows, depth), key.dtype),
            pltpu.SemaphoreType.DMA((2, heads)),
        ],
        compiler_params=pltpu.CompilerParams(vmem_limit_bytes=24 * 1024 * 1024),
    )(order, filled, key, value)


def hop_kernel(
    level, count, packed, time_ref, hidden, modulation, weight, latents, arrived, moved, shaped, send_sem, recv_sem
):
    ways = 2
    heads = packed.shape[1]
    me = lax.axis_index("seq")
    caps = (0, level, min(heads, level * 3 // 2), min(heads, level * 2))

    def cap(dests):
        value = jnp.int32(0)
        for number in range(1, count):
            value = jnp.where(dests == number, min(caps[number], heads), value)
        return value

    incoming = (cap(count - me), cap(me + 1))
    outgoing = (cap(count - 1 - me), cap(me))
    targets = (me + 1, me - 1)
    has_target = (me < count - 1, me > 0)

    def source_exists(way, hop):
        return me >= hop if way == 0 else me + hop < count

    def hop_copy(way, hop, index, source):
        origin = packed.at[way, index] if hop == 1 else arrived.at[source, index]
        return pltpu.make_async_remote_copy(
            src_ref=origin,
            dst_ref=arrived.at[source, index],
            send_sem=send_sem.at[way, hop - 1, index],
            recv_sem=recv_sem.at[way, hop - 1, index],
            device_id={"seq": targets[way]},
            device_id_type=pl.DeviceIdType.MESH,
        )

    def back(way, hops):
        return me - hops if way == 0 else me + hops

    barrier = pltpu.get_barrier_semaphore()
    for way in range(ways):
        @pl.when(has_target[way])
        def _():
            pl.semaphore_signal(
                barrier, inc=1, device_id={"seq": targets[way]}, device_id_type=pl.DeviceIdType.MESH
            )
    pl.semaphore_wait(barrier, jnp.where((me == 0) | (me == count - 1), 1, 2))

    def launch(index, carry):
        for way in range(ways):
            @pl.when(index < outgoing[way])
            def _():
                hop_copy(way, 1, index, me).start()
        return carry

    lax.fori_loop(0, jnp.maximum(outgoing[0], outgoing[1]), launch, 0)

    def shape_rows(step, carry):
        part = pl.ds(pl.multiple_of(step * ROWS, ROWS), ROWS)
        source = hidden[part, :].astype(jnp.float32)
        centred = source - jnp.mean(source, axis=1, keepdims=True)
        spread = jnp.mean(centred * centred, axis=1, keepdims=True)
        normed = centred * lax.rsqrt(spread + epsilon)
        shaped[part, :] = (normed * (1.0 + modulation[1:2, :]) + modulation[0:1, :]).astype(jnp.bfloat16)
        return carry

    lax.fori_loop(0, hidden.shape[0] // ROWS, shape_rows, 0)
    velocity = jnp.dot(shaped[...], weight[...], preferred_element_type=jnp.float32)
    now = jnp.full((1, latents.shape[1]), time_ref[0], jnp.int32)
    change = noise_level(now - 1) - noise_level(now)
    moved[...] = (latents[...] + change * velocity).astype(jnp.bfloat16)

    for hop in range(1, count - 1):
        def pass_on(index, carry):
            for way in range(ways):
                @pl.when(source_exists(way, hop) & (index < outgoing[way]))
                def _():
                    hop_copy(way, hop, index, back(way, hop)).wait_recv()
                    hop_copy(way, hop + 1, index, back(way, hop)).start()
            return carry

        lax.fori_loop(0, jnp.maximum(outgoing[0], outgoing[1]), pass_on, 0)

    for hop in range(1, count):
        def take(index, carry):
            for way in range(ways):
                kept = source_exists(way, hop) & (index < incoming[way])
                if hop < count - 1:
                    kept = kept & (index >= outgoing[way])

                @pl.when(kept)
                def _():
                    hop_copy(way, hop, index, back(way, hop)).wait_recv()
            return carry

        lax.fori_loop(0, jnp.maximum(incoming[0], incoming[1]), take, 0)

    for hop in range(1, count):
        def drain(index, carry):
            for way in range(ways):
                sends = index < outgoing[way]
                if hop > 1:
                    sends = sends & source_exists(way, hop - 1)

                @pl.when(sends)
                def _():
                    hop_copy(way, hop, index, back(way, hop - 1)).wait_send()
            return carry

        lax.fori_loop(0, jnp.maximum(outgoing[0], outgoing[1]), drain, 0)


def hop_call(level, collective, count, packed, time_index, hidden, modulation, weight, latents):
    _, heads, _, rows, depth = packed.shape
    anywhere = pl.BlockSpec(memory_space=pl.ANY)
    vmem = pl.BlockSpec(memory_space=pltpu.VMEM)
    return pl.pallas_call(
        functools.partial(hop_kernel, level, count),
        out_shape=(
            jax.ShapeDtypeStruct((count, heads, 2, rows, depth), packed.dtype),
            jax.ShapeDtypeStruct(latents.shape, jnp.bfloat16),
        ),
        in_specs=[anywhere, pl.BlockSpec(memory_space=pltpu.SMEM), vmem, vmem, vmem, vmem],
        out_specs=(anywhere, vmem),
        scratch_shapes=[
            pltpu.VMEM(hidden.shape, jnp.bfloat16),
            pltpu.SemaphoreType.DMA((2, count - 1, heads)),
            pltpu.SemaphoreType.DMA((2, count - 1, heads)),
        ],
        compiler_params=pltpu.CompilerParams(
            collective_id=collective, has_side_effects=True, vmem_limit_bytes=24 * 1024 * 1024
        ),
    )(packed, time_index, hidden, modulation, weight, latents)


def attend_kernel(slot, bias, q_ref, k_ref, v_ref, arrived, out_ref):
    count, heads, _, rows, depth = arrived.shape
    me = lax.axis_index("seq")
    scale = depth ** (-0.5)

    def attend(step, carry):
        results = []
        for offset in range(GROUP):
            head = step * GROUP + offset
            cols = pl.ds(pl.multiple_of(head * depth, depth), depth)
            query = q_ref[:, cols]
            keys, values, adds = [k_ref[:, cols]], [v_ref[:, cols]], [jnp.float32(0)]
            for step_away in range(1, count):
                source = lax.rem(me + step_away, count)
                keys.append(arrived[source, slot[source, head], 0])
                values.append(arrived[source, slot[source, head], 1])
                adds.append(bias[source, head])
            scores = [
                scale * lax.dot_general(
                    query, one, (((1,), (1,)), ((), ())), preferred_element_type=jnp.float32
                ) + add
                for one, add in zip(keys, adds)
            ]
            top = jnp.max(functools.reduce(jnp.maximum, scores), axis=1, keepdims=True)
            weights = [jnp.exp(one - top) for one in scores]
            part = jnp.sum(sum(weights), axis=1, keepdims=True)
            mixed = jnp.dot(
                jnp.concatenate([one.astype(jnp.bfloat16) for one in weights], axis=1),
                jnp.concatenate(values, axis=0),
                preferred_element_type=jnp.float32,
            )
            results.append((cols, (mixed / part).astype(jnp.bfloat16)))
        for cols, value in results:
            out_ref[:, cols] = value
        return carry

    lax.fori_loop(0, heads // GROUP, attend, 0)


def attend_call(slot, bias, query, key, value, arrived):
    rows, width = query.shape
    count = arrived.shape[0]
    smem = pl.BlockSpec(memory_space=pltpu.SMEM)
    vmem = pl.BlockSpec(memory_space=pltpu.VMEM)
    return pl.pallas_call(
        attend_kernel,
        out_shape=jax.ShapeDtypeStruct(query.shape, jnp.bfloat16),
        in_specs=[smem, smem, vmem, vmem, vmem, vmem],
        out_specs=vmem,
        compiler_params=pltpu.CompilerParams(vmem_limit_bytes=32 * 1024 * 1024),
        cost_estimate=pl.CostEstimate(
            flops=4 * count * rows * rows * width,
            bytes_accessed=8 * rows * width + 4 * count * rows * width,
            transcendentals=count * rows * width,
        ),
    )(slot, bias, query, key, value, arrived)


def local_by_blocks(
    query_rows,
    key_rows,
    value_rows,
    hidden_state,
    modulation,
    head_weight,
    latents,
    time_index,
    live_counts,
    block_lists,
):
    count = lax.axis_size("seq")
    me = lax.axis_index("seq")
    heads = live_counts.shape[0]
    order, filled, slot, bias, most = hop_tables(live_counts, block_lists, count, me)
    levels = tuple(level for level in LEVELS if level < heads) + (heads,)
    chosen = jnp.int32(0)
    for level in levels[:-1]:
        over = (most[1] > level) | (most[2] > level * 3 // 2) | (most[3] > level * 2)
        chosen = chosen + over.astype(jnp.int32)
    calls = [
        functools.partial(hop_call, level, number, count) for number, level in enumerate(levels)
    ]
    packed = pack_call(order, filled, key_rows[0], value_rows[0], heads)
    arrived, moved = lax.switch(
        chosen, calls, packed, time_index, hidden_state[0], modulation[0], head_weight, latents[0]
    )
    queue_next = passed_along(moved[None], "queue", -1).astype(jnp.float32)
    attended = attend_call(slot, bias, query_rows[0], key_rows[0], value_rows[0], arrived)
    return (attended[None], queue_next)


def solution(mesh):
    seq_count = mesh.shape["seq"]

    def local(*arrays):
        blocks = arrays[8].shape[1]
        fits = seq_count <= 4 and blocks == seq_count and arrays[0].shape[1] == arrays[0].shape[2] // arrays[8].shape[0]
        return (local_by_blocks if fits else local_by_heads)(*arrays)

    placed = (
        P(("groups", "queue"), "seq", None),
        P(("groups", "queue"), "seq", None),
        P(("groups", "queue"), "seq", None),
        P(("groups", "queue"), "seq", None),
        P(("groups", "queue"), None, None),
        P(),
        P(("groups", "queue"), "seq", None),
        P(("groups", "queue")),
        P(),
        P(),
    )
    return jax.shard_map(
        local,
        mesh=mesh,
        in_specs=placed,
        out_specs=(P(("groups", "queue"), "seq", None), P(("groups", "queue"), "seq", None)),
        check_vma=False,
    )
```

```python
import functools

import jax
import jax.numpy as jnp
from jax import lax
from jax.experimental import pallas as pl
from jax.experimental.pallas import tpu as pltpu
from jax.sharding import PartitionSpec as P

STEPS = 8


epsilon = 1e-06
plan_shift = 5.0


def passed_along(value, axis, steps):
    count = lax.axis_size(axis)
    pairs = [(source, (source + steps) % count) for source in range(count)]
    return lax.ppermute(value, axis, pairs)


def noise_level(step_value):
    fraction = step_value.astype(jnp.float32) / STEPS
    return plan_shift * fraction / (1.0 + (plan_shift - 1.0) * fraction)


def attend(query_head, key_head, value_head, live, blocks):
    block_total = live.shape[0]
    block_size = query_head.shape[0] // block_total
    head_depth = query_head.shape[1]
    slot_total = blocks.shape[1]
    query_blocks = query_head.reshape(block_total, block_size, head_depth)
    key_blocks = key_head.reshape(-1, block_size, head_depth)
    value_blocks = value_head.reshape(-1, block_size, head_depth)
    scale = head_depth ** (-0.5)

    def advance(slot_number, state_now):
        highest, totals, summed = state_now
        chosen = lax.dynamic_index_in_dim(blocks, slot_number, 1, keepdims=False)
        key_chosen = jnp.take(key_blocks, chosen, axis=0)
        value_chosen = jnp.take(value_blocks, chosen, axis=0)
        scores = (
            jnp.einsum("bid,bjd->bij", query_blocks, key_chosen, preferred_element_type=jnp.float32)
            * scale
        )
        active = (slot_number < live)[:, None]
        new_highest = jnp.where(active, jnp.maximum(highest, jnp.max(scores, axis=2)), highest)
        weights = jnp.exp(scores - new_highest[:, :, None])
        factor = jnp.exp(highest - new_highest)
        new_totals = jnp.where(active, totals * factor + jnp.sum(weights, axis=2), totals)
        mixed = jnp.einsum(
            "bij,bjd->bid",
            weights.astype(jnp.bfloat16),
            value_chosen,
            preferred_element_type=jnp.float32,
        )
        new_summed = jnp.where(active[:, :, None], summed * factor[:, :, None] + mixed, summed)
        return (new_highest, new_totals, new_summed)

    start_state = (
        jnp.full((block_total, block_size), -jnp.inf, jnp.float32),
        jnp.zeros((block_total, block_size), jnp.float32),
        jnp.zeros((block_total, block_size, head_depth), jnp.float32),
    )
    final_state = lax.fori_loop(0, slot_total, advance, start_state)
    result = (final_state[2] / final_state[1][:, :, None]).astype(jnp.bfloat16)
    return result.reshape(block_total * block_size, head_depth)


def attend_heads(query_cols, key_cols, value_cols, head_ids, live_counts, block_lists):
    head_total = head_ids.shape[0]
    head_depth = query_cols.shape[1] // head_total
    query_stack = jnp.transpose(
        query_cols.reshape(query_cols.shape[0], head_total, head_depth), (1, 0, 2)
    )
    key_stack = jnp.transpose(
        key_cols.reshape(key_cols.shape[0], head_total, head_depth), (1, 0, 2)
    )
    value_stack = jnp.transpose(
        value_cols.reshape(value_cols.shape[0], head_total, head_depth), (1, 0, 2)
    )
    live_heads = jnp.take(live_counts, head_ids, axis=0)
    list_heads = jnp.take(block_lists, head_ids, axis=0)
    results = jax.vmap(attend)(query_stack, key_stack, value_stack, live_heads, list_heads)
    return jnp.transpose(results, (1, 0, 2)).reshape(query_cols.shape[0], head_total * head_depth)


def next_latents(hidden_state, modulation, head_weight, latents, time_index):
    source = hidden_state[0].astype(jnp.float32)
    mean_row = jnp.mean(source, axis=1, keepdims=True)
    centred = source - mean_row
    spread = jnp.mean(centred * centred, axis=1, keepdims=True)
    normed = centred * lax.rsqrt(spread + epsilon)
    shaped = (normed * (1.0 + modulation[0, 1]) + modulation[0, 0]).astype(jnp.bfloat16)
    velocity = jnp.dot(shaped, head_weight, preferred_element_type=jnp.float32)
    change = noise_level(time_index[0] - 1) - noise_level(time_index[0])
    moved = latents[0] + change * velocity
    return passed_along(moved[None].astype(jnp.bfloat16), "queue", -1).astype(jnp.float32)


def local_by_heads(
    query_rows,
    key_rows,
    value_rows,
    hidden_state,
    modulation,
    head_weight,
    latents,
    time_index,
    live_counts,
    block_lists,
):
    seq_count = lax.axis_size("seq")
    own_index = lax.axis_index("seq")
    head_count = live_counts.shape[0]
    per_device = head_count // seq_count
    order = jnp.arange(head_count, dtype=jnp.int32)
    query_send, key_send, value_send = (query_rows, key_rows, value_rows)
    query_heads, key_heads, value_heads = (
        lax.all_to_all(query_send, "seq", split_axis=2, concat_axis=1, tiled=True),
        lax.all_to_all(key_send, "seq", split_axis=2, concat_axis=1, tiled=True),
        lax.all_to_all(value_send, "seq", split_axis=2, concat_axis=1, tiled=True),
    )
    queue_next = next_latents(hidden_state, modulation, head_weight, latents, time_index)
    query_cols = query_heads[0]
    key_cols = key_heads[0]
    value_cols = value_heads[0]
    own_ids = lax.dynamic_slice_in_dim(order, own_index * per_device, per_device, 0)
    attended = attend_heads(query_cols, key_cols, value_cols, own_ids, live_counts, block_lists)
    mixed_back = lax.all_to_all(attended[None], "seq", split_axis=1, concat_axis=2, tiled=True)
    return (mixed_back, queue_next)


LEVELS = (12, 13, 14, 15, 16, 17, 18, 21)
GROUP = 2
ROWS = 16


def hop_tables(live_counts, block_lists, count, me):
    heads = live_counts.shape[0]
    spots = jnp.arange(count, dtype=jnp.int32)
    live = jnp.arange(block_lists.shape[2], dtype=jnp.int32)[None, None, :] < live_counts[:, :, None]
    need = jnp.any((block_lists[..., None] == spots) & live[..., None], axis=2)
    away = spots[:, None] - spots[None, :]
    reach = jnp.stack(
        [
            jnp.max(jnp.where(need, jnp.maximum(away, 0)[None], 0), axis=1),
            jnp.max(jnp.where(need, jnp.maximum(-away, 0)[None], 0), axis=1),
        ]
    ).transpose(0, 2, 1)
    numbers = jnp.arange(heads, dtype=jnp.int32)
    rank = reach * heads + (heads - 1 - numbers)
    place = jnp.sum((rank[..., None, :] > rank[..., :, None]).astype(jnp.int32), axis=-1)
    own_place = lax.dynamic_index_in_dim(place, me, 1, keepdims=False)
    order = jnp.sum(
        jnp.where(own_place[:, None, :] == numbers[None, :, None], numbers[None, None, :], 0), axis=-1
    )
    own_need = lax.dynamic_index_in_dim(need, me, 1, keepdims=False) & (spots != me)
    slot = jnp.where(own_need.T, jnp.where((spots < me)[:, None], place[0], place[1]), 0)
    bias = jnp.where(own_need.T, 0.0, -jnp.inf).astype(jnp.float32)
    filled = jnp.sum((lax.dynamic_index_in_dim(reach, me, 1, keepdims=False) > 0).astype(jnp.int32), axis=-1)
    most = {1: jnp.int32(0), 2: jnp.int32(0), 3: jnp.int32(0)}
    for side in range(2):
        for source in range(count):
            for hop in range(1, count):
                left = count - source - hop if side == 0 else source - hop + 1
                if left in most:
                    carried = jnp.sum((reach[side, source] >= hop).astype(jnp.int32))
                    most[left] = jnp.maximum(most[left], carried)
    return order.astype(jnp.int32), filled, slot.astype(jnp.int32), bias, most


def pack_kernel(order, filled, k_ref, v_ref, packed, staged, sem):
    _, heads, _, rows, depth = packed.shape

    def copy(way, index):
        return pltpu.make_async_copy(staged.at[way, index], packed.at[way, index], sem.at[way, index])

    def begin(index, carry):
        for way in range(2):
            @pl.when(index < jnp.maximum(filled[way], 1))
            def _():
                head = order[way, index]
                cols = pl.ds(pl.multiple_of(head * depth, depth), depth)
                staged[way, index, 0] = k_ref[:, cols]
                staged[way, index, 1] = v_ref[:, cols]
                copy(way, index).start()
        return carry

    def end(index, carry):
        for way in range(2):
            @pl.when(index < jnp.maximum(filled[way], 1))
            def _():
                copy(way, index).wait()
        return carry

    lax.fori_loop(0, heads, begin, 0)
    lax.fori_loop(0, heads, end, 0)


def pack_call(order, filled, key, value, heads):
    rows, width = key.shape
    depth = width // heads
    smem = pl.BlockSpec(memory_space=pltpu.SMEM)
    vmem = pl.BlockSpec(memory_space=pltpu.VMEM)
    return pl.pallas_call(
        pack_kernel,
        out_shape=jax.ShapeDtypeStruct((2, heads, 2, rows, depth), key.dtype),
        in_specs=[smem, smem, vmem, vmem],
        out_specs=pl.BlockSpec(memory_space=pl.ANY),
        scratch_shapes=[
            pltpu.VMEM((2, heads, 2, rows, depth), key.dtype),
            pltpu.SemaphoreType.DMA((2, heads)),
        ],
        compiler_params=pltpu.CompilerParams(vmem_limit_bytes=24 * 1024 * 1024),
    )(order, filled, key, value)


def hop_kernel(
    level, count, packed, time_ref, hidden, modulation, weight, latents, arrived, moved, shaped, send_sem, recv_sem
):
    ways = 2
    heads = packed.shape[1]
    me = lax.axis_index("seq")
    caps = (0, level, min(heads, level * 3 // 2), min(heads, level * 2))

    def cap(dests):
        value = jnp.int32(0)
        for number in range(1, count):
            value = jnp.where(dests == number, min(caps[number], heads), value)
        return value

    incoming = (cap(count - me), cap(me + 1))
    outgoing = (cap(count - 1 - me), cap(me))
    targets = (me + 1, me - 1)
    has_target = (me < count - 1, me > 0)

    def source_exists(way, hop):
        return me >= hop if way == 0 else me + hop < count

    def hop_copy(way, hop, index, source):
        origin = packed.at[way, index] if hop == 1 else arrived.at[source, index]
        return pltpu.make_async_remote_copy(
            src_ref=origin,
            dst_ref=arrived.at[source, index],
            send_sem=send_sem.at[way, hop - 1, index],
            recv_sem=recv_sem.at[way, hop - 1, index],
            device_id={"seq": targets[way]},
            device_id_type=pl.DeviceIdType.MESH,
        )

    def back(way, hops):
        return me - hops if way == 0 else me + hops

    barrier = pltpu.get_barrier_semaphore()
    for way in range(ways):
        @pl.when(has_target[way])
        def _():
            pl.semaphore_signal(
                barrier, inc=1, device_id={"seq": targets[way]}, device_id_type=pl.DeviceIdType.MESH
            )
    pl.semaphore_wait(barrier, jnp.where((me == 0) | (me == count - 1), 1, 2))

    def launch(index, carry):
        for way in range(ways):
            @pl.when(index < outgoing[way])
            def _():
                hop_copy(way, 1, index, me).start()
        return carry

    lax.fori_loop(0, jnp.maximum(outgoing[0], outgoing[1]), launch, 0)

    def shape_rows(step, carry):
        part = pl.ds(pl.multiple_of(step * ROWS, ROWS), ROWS)
        source = hidden[part, :].astype(jnp.float32)
        centred = source - jnp.mean(source, axis=1, keepdims=True)
        spread = jnp.mean(centred * centred, axis=1, keepdims=True)
        normed = centred * lax.rsqrt(spread + epsilon)
        shaped[part, :] = (normed * (1.0 + modulation[1:2, :]) + modulation[0:1, :]).astype(jnp.bfloat16)
        return carry

    lax.fori_loop(0, hidden.shape[0] // ROWS, shape_rows, 0)
    velocity = jnp.dot(shaped[...], weight[...], preferred_element_type=jnp.float32)
    now = jnp.full((1, latents.shape[1]), time_ref[0], jnp.int32)
    change = noise_level(now - 1) - noise_level(now)
    moved[...] = (latents[...] + change * velocity).astype(jnp.bfloat16)

    for hop in range(1, count - 1):
        def pass_on(index, carry):
            for way in range(ways):
                @pl.when(source_exists(way, hop) & (index < outgoing[way]))
                def _():
                    hop_copy(way, hop, index, back(way, hop)).wait_recv()
                    hop_copy(way, hop + 1, index, back(way, hop)).start()
            return carry

        lax.fori_loop(0, jnp.maximum(outgoing[0], outgoing[1]), pass_on, 0)

    for hop in range(1, count):
        def take(index, carry):
            for way in range(ways):
                kept = source_exists(way, hop) & (index < incoming[way])
                if hop < count - 1:
                    kept = kept & (index >= outgoing[way])

                @pl.when(kept)
                def _():
                    hop_copy(way, hop, index, back(way, hop)).wait_recv()
            return carry

        lax.fori_loop(0, jnp.maximum(incoming[0], incoming[1]), take, 0)

    for hop in range(1, count):
        def drain(index, carry):
            for way in range(ways):
                sends = index < outgoing[way]
                if hop > 1:
                    sends = sends & source_exists(way, hop - 1)

                @pl.when(sends)
                def _():
                    hop_copy(way, hop, index, back(way, hop - 1)).wait_send()
            return carry

        lax.fori_loop(0, jnp.maximum(outgoing[0], outgoing[1]), drain, 0)


def hop_call(level, collective, count, packed, time_index, hidden, modulation, weight, latents):
    _, heads, _, rows, depth = packed.shape
    anywhere = pl.BlockSpec(memory_space=pl.ANY)
    vmem = pl.BlockSpec(memory_space=pltpu.VMEM)
    return pl.pallas_call(
        functools.partial(hop_kernel, level, count),
        out_shape=(
            jax.ShapeDtypeStruct((count, heads, 2, rows, depth), packed.dtype),
            jax.ShapeDtypeStruct(latents.shape, jnp.bfloat16),
        ),
        in_specs=[anywhere, pl.BlockSpec(memory_space=pltpu.SMEM), vmem, vmem, vmem, vmem],
        out_specs=(anywhere, vmem),
        scratch_shapes=[
            pltpu.VMEM(hidden.shape, jnp.bfloat16),
            pltpu.SemaphoreType.DMA((2, count - 1, heads)),
            pltpu.SemaphoreType.DMA((2, count - 1, heads)),
        ],
        compiler_params=pltpu.CompilerParams(
            collective_id=collective, has_side_effects=True, vmem_limit_bytes=24 * 1024 * 1024
        ),
    )(packed, time_index, hidden, modulation, weight, latents)


def attend_kernel(slot, bias, q_ref, k_ref, v_ref, arrived, out_ref):
    count, heads, _, rows, depth = arrived.shape
    me = lax.axis_index("seq")
    scale = depth ** (-0.5)

    def attend(step, carry):
        results = []
        for offset in range(GROUP):
            head = step * GROUP + offset
            cols = pl.ds(pl.multiple_of(head * depth, depth), depth)
            query = q_ref[:, cols]
            keys, values, adds = [k_ref[:, cols]], [v_ref[:, cols]], [jnp.float32(0)]
            for step_away in range(1, count):
                source = lax.rem(me + step_away, count)
                keys.append(arrived[source, slot[source, head], 0])
                values.append(arrived[source, slot[source, head], 1])
                adds.append(bias[source, head])
            scores = [
                scale * lax.dot_general(
                    query, one, (((1,), (1,)), ((), ())), preferred_element_type=jnp.float32
                ) + add
                for one, add in zip(keys, adds)
            ]
            top = jnp.max(functools.reduce(jnp.maximum, scores), axis=1, keepdims=True)
            weights = [jnp.exp(one - top) for one in scores]
            part = jnp.sum(sum(weights), axis=1, keepdims=True)
            mixed = jnp.dot(
                jnp.concatenate([one.astype(jnp.bfloat16) for one in weights], axis=1),
                jnp.concatenate(values, axis=0),
                preferred_element_type=jnp.float32,
            )
            results.append((cols, (mixed / part).astype(jnp.bfloat16)))
        for cols, value in results:
            out_ref[:, cols] = value
        return carry

    lax.fori_loop(0, heads // GROUP, attend, 0)


def attend_call(slot, bias, query, key, value, arrived):
    rows, width = query.shape
    count = arrived.shape[0]
    smem = pl.BlockSpec(memory_space=pltpu.SMEM)
    vmem = pl.BlockSpec(memory_space=pltpu.VMEM)
    return pl.pallas_call(
        attend_kernel,
        out_shape=jax.ShapeDtypeStruct(query.shape, jnp.bfloat16),
        in_specs=[smem, smem, vmem, vmem, vmem, vmem],
        out_specs=vmem,
        compiler_params=pltpu.CompilerParams(vmem_limit_bytes=32 * 1024 * 1024),
        cost_estimate=pl.CostEstimate(
            flops=4 * count * rows * rows * width,
            bytes_accessed=8 * rows * width + 4 * count * rows * width,
            transcendentals=count * rows * width,
        ),
    )(slot, bias, query, key, value, arrived)


def local_by_blocks(
    query_rows,
    key_rows,
    value_rows,
    hidden_state,
    modulation,
    head_weight,
    latents,
    time_index,
    live_counts,
    block_lists,
):
    count = lax.axis_size("seq")
    me = lax.axis_index("seq")
    heads = live_counts.shape[0]
    order, filled, slot, bias, most = hop_tables(live_counts, block_lists, count, me)
    levels = tuple(level for level in LEVELS if level < heads) + (heads,)
    chosen = jnp.int32(0)
    for level in levels[:-1]:
        over = (most[1] > level) | (most[2] > level * 3 // 2) | (most[3] > level * 2)
        chosen = chosen + over.astype(jnp.int32)
    calls = [
        functools.partial(hop_call, level, number, count) for number, level in enumerate(levels)
    ]
    packed = pack_call(order, filled, key_rows[0], value_rows[0], heads)
    arrived, moved = lax.switch(
        chosen, calls, packed, time_index, hidden_state[0], modulation[0], head_weight, latents[0]
    )
    queue_next = passed_along(moved[None], "queue", -1).astype(jnp.float32)
    attended = attend_call(slot, bias, query_rows[0], key_rows[0], value_rows[0], arrived)
    return (attended[None], queue_next)


def solution(mesh):
    seq_count = mesh.shape["seq"]

    def local(*arrays):
        blocks = arrays[8].shape[1]
        fits = seq_count <= 4 and blocks == seq_count and arrays[0].shape[1] == arrays[0].shape[2] // arrays[8].shape[0]
        return (local_by_blocks if fits else local_by_heads)(*arrays)

    placed = (
        P(("groups", "queue"), "seq", None),
        P(("groups", "queue"), "seq", None),
        P(("groups", "queue"), "seq", None),
        P(("groups", "queue"), "seq", None),
        P(("groups", "queue"), None, None),
        P(),
        P(("groups", "queue"), "seq", None),
        P(("groups", "queue")),
        P(),
        P(),
    )
    return jax.shard_map(
        local,
        mesh=mesh,
        in_specs=placed,
        out_specs=(P(("groups", "queue"), "seq", None), P(("groups", "queue"), "seq", None)),
        check_vma=False,
    )
```
